32 devices in a mesh: group: 2 (over y), seq: 4 (over z), img: 2 (over x), tp: 2 (over core).
Axes of the slice: x: 2, y: 2, z: 4, core: 2. Of those that a mesh axis runs over, the one named last changes fastest.
Arguments:
- rotated_queries: bfloat16 [16, 2048, 2048], P(('group', 'img'), 'seq', 'tp'), parts along dimension 0, may hold values from -90 to 90
- rotated_keys: bfloat16 [16, 2048, 2048], P(('group', 'img'), 'seq', 'tp'), parts along dimension 0, may hold values from -7.5 to 7.5
- head_values: bfloat16 [16, 2048, 2048], P(('group', 'img'), 'seq', 'tp'), parts along dimension 0, may hold values from -6 to 6
- residual: bfloat16 [16, 2048, 3072], P(('group', 'img'), 'seq', 'tp'), parts along dimension 0, may hold values from -6 to 6
- image_gate: bfloat16 [16, 3072], P(('group', 'img'), 'tp'), parts along dimension 0, may hold values from 0.5 to 1.5
- output_weight: bfloat16 [2048, 3072], P('tp', 'seq'), may hold values from -0.75 to 0.75
- adapter_down: bfloat16 [1024, 2048, 64], P(('group', 'seq', 'img'), 'tp'), parts along dimension 0, may hold values from -0.75 to 0.75
- adapter_up: bfloat16 [1024, 64, 3072], P(('group', 'seq', 'img'), None, 'tp'), parts along dimension 0, may hold values from -0.75 to 0.75
- image_group: int32 [16], P('group'), parts along dimension 0, may hold values from 0 to 3, as said below
- group_adapter: int32 [8], P('group'), parts along dimension 0, may hold values from 0 to 511, as said below
- adapter_store_row: int32 [1024], P('group'), parts along dimension 0, may hold values from 0 to 511, each once
Outputs:
- updated: bfloat16 [16, 2048, 3072], P(('group', 'img'), 'seq', 'tp'), parts along dimension 0
The draws below stay inside these ranges and needn't reach their ends.
There are 2 independent parts, one for each index of `group`. The reference program is written for one: setup_inputs(seed, part) draws one part's arguments, and reference() takes and returns one part's arrays. A program takes and returns all parts, laid end to end along the dimension named above; an argument that names none is the same for every part. Nothing has to cross between parts.
Inputs may be any that keep to these rules, and one draw needn't show every extreme that they name: `image_group`: every group number from 0 to 3 is used by at least one image. `group_adapter`: the 4 adapter ids are distinct. A permutation: adapter a is row adapter_store_row[a] of adapter_down and adapter_up.
All inputs are finite; a program needn't handle non-finite values.
Results may differ from the reference program's by a relative error of at most 0.0048.
Values may be sent and summed in bfloat16 or wider, within the bound.
No kernel may reach another device: no remote copies, remote signals or barrier semaphores. Data moves between devices by JAX's collectives and lax.ppermute only.
A program may use at most 192 MiB of HBM per device.

```python
import jax
import jax.numpy as jnp
from jax import lax

MODEL_WIDTH = 3072
LOCAL_HEADS = 16
HEAD_WIDTH = 128
ADAPTER_RANK = 64
ADAPTER_COUNT = 512
S = 2048
IMAGES = 8
SLOTS = 4


def paired_rows(key):
    array_shape = (IMAGES, S, LOCAL_HEADS * HEAD_WIDTH)
    queries = 1.4 * jax.random.truncated_normal(jax.random.fold_in(key, 21), -5.0, 5.0, array_shape, jnp.float32)
    keys_base = 1.4 * jax.random.truncated_normal(jax.random.fold_in(key, 22), -5.0, 5.0, array_shape, jnp.float32)
    return (queries, keys_base)


def draw_rotated_queries(key, part):
    queries, keys_base = paired_rows(key)
    return queries.astype(jnp.bfloat16)


def draw_rotated_keys(key, part):
    queries, keys_base = paired_rows(key)
    return keys_base.astype(jnp.bfloat16)


def draw_image_group(key, part):
    key = jax.random.fold_in(key, 31)
    spread = jax.random.randint(jax.random.fold_in(key, 1), (IMAGES - SLOTS,), 0, max(SLOTS // 4, 1))
    listed = jnp.concatenate([jnp.arange(SLOTS), spread]).astype(jnp.int32)
    order = jax.random.permutation(jax.random.fold_in(key, 2), IMAGES)
    return listed[order].astype(jnp.int32)


def draw_group_adapter(key, part):
    key = jax.random.fold_in(key, 41)
    return jax.random.permutation(key, ADAPTER_COUNT)[:SLOTS].astype(jnp.int32)


def steps_of(key, shape, cuts, low, high):
    factor_of = 1.0
    for dim, blocks in cuts:
        draws = jax.random.uniform(jax.random.fold_in(jax.random.fold_in(key, 6), dim), (blocks,), jnp.float32, low / len(cuts), high / len(cuts))
        factor_of = factor_of * jnp.repeat(jnp.exp(draws), shape[dim] // blocks).reshape((-1,) + (1,) * (len(shape) - 1 - dim))
    return factor_of


def centred(rng, shape, scale, reach, cuts=(), held_as=jnp.bfloat16):
    loudness = steps_of(rng, shape, cuts, -0.22, 0.18) if cuts else 1.0
    values = jax.random.normal(rng, shape, jnp.float32) * scale * loudness
    return jnp.minimum(jnp.maximum(values, -reach), reach).astype(held_as)


def setup_inputs(seed: int = 0, part: int = 0) -> dict:
    seeds = jax.random.split(jax.random.key(seed), 12)
    part_splits = jax.random.split(jax.random.fold_in(seeds[11], part), 12)
    return {
        "rotated_queries": draw_rotated_queries(jax.random.fold_in(jax.random.fold_in(seeds[11], part), 71), part),
        "rotated_keys": draw_rotated_keys(jax.random.fold_in(jax.random.fold_in(seeds[11], part), 71), part),
        "head_values": centred(part_splits[2], (IMAGES, S, LOCAL_HEADS * HEAD_WIDTH), 1.0, 6.0, ((0, 2), (1, 4), (2, 2))),
        "residual": centred(part_splits[3], (IMAGES, S, MODEL_WIDTH), 1.0, 6.0, ((0, 2), (1, 4), (2, 2))),
        "image_gate": jnp.clip(0.5 + 1.0 * jax.random.uniform(part_splits[4], (IMAGES, MODEL_WIDTH), jnp.float32) ** steps_of(part_splits[4], (IMAGES, MODEL_WIDTH), ((0, 2), (1, 2)), -0.2, 0.2), 0.5, 1.5).astype(jnp.bfloat16),
        "output_weight": centred(seeds[5], (LOCAL_HEADS * HEAD_WIDTH, MODEL_WIDTH), (LOCAL_HEADS * HEAD_WIDTH // 32) ** -0.5, 0.75, ((0, 2), (1, 4))),
        "adapter_down": centred(part_splits[6], (ADAPTER_COUNT, LOCAL_HEADS * HEAD_WIDTH, ADAPTER_RANK), (LOCAL_HEADS * HEAD_WIDTH // 32) ** -0.5, 0.75, ((0, 8), (1, 2))),
        "adapter_up": centred(part_splits[7], (ADAPTER_COUNT, ADAPTER_RANK, MODEL_WIDTH), ADAPTER_RANK ** -0.5, 0.75, ((0, 8), (2, 2))),
        "image_group": draw_image_group(jax.random.fold_in(jax.random.fold_in(seeds[11], part), 71), part),
        "group_adapter": draw_group_adapter(jax.random.fold_in(jax.random.fold_in(seeds[11], part), 71), part),
        "adapter_store_row": jax.random.permutation(part_splits[10], ADAPTER_COUNT).astype(jnp.int32),
    }


def attend_one(query_head, key_head, value_head):
    length = query_head.shape[0]
    block_rows = min(512, length)
    scale = query_head.shape[1] ** -0.5

    def one_block(query_block):
        scores = jnp.dot(query_block, key_head.T, preferred_element_type=jnp.float32) * scale
        largest = jnp.max(scores, axis=1, keepdims=True)
        exponent = jnp.exp(scores - largest)
        totals = jnp.sum(exponent, axis=1, keepdims=True)
        weights = exponent.astype(jnp.bfloat16)
        return (jnp.dot(weights, value_head, preferred_element_type=jnp.float32) / totals).astype(jnp.bfloat16)

    blocks = query_head.reshape(length // block_rows, block_rows, query_head.shape[1])
    return lax.map(one_block, blocks).reshape(length, query_head.shape[1])


def split_heads(array):
    return array.reshape(IMAGES, S, LOCAL_HEADS, HEAD_WIDTH).transpose(0, 2, 1, 3).reshape(IMAGES * LOCAL_HEADS, S, HEAD_WIDTH)


def reference(rotated_queries, rotated_keys, head_values, residual, image_gate, output_weight, adapter_down, adapter_up, image_group, group_adapter, adapter_store_row):
    heads_out = lax.map(lambda triple: attend_one(*triple), (split_heads(rotated_queries), split_heads(rotated_keys), split_heads(head_values)))
    attended = heads_out.reshape(IMAGES, LOCAL_HEADS, S, HEAD_WIDTH).transpose(0, 2, 1, 3).reshape(IMAGES, S, LOCAL_HEADS * HEAD_WIDTH)
    projected = jnp.dot(attended.reshape(IMAGES * S, LOCAL_HEADS * HEAD_WIDTH), output_weight, preferred_element_type=jnp.float32).reshape(IMAGES, S, MODEL_WIDTH)
    store_row_count = adapter_store_row[group_adapter[image_group]].astype(jnp.int32)
    down_matrix = adapter_down[store_row_count].astype(jnp.float32)
    up_matrix = adapter_up[store_row_count].astype(jnp.float32)
    inner_terms = jnp.einsum('bsh,bhr->bsr', attended.astype(jnp.float32), down_matrix).astype(jnp.bfloat16)
    adapted = jnp.einsum('bsr,brd->bsd', inner_terms.astype(jnp.float32), up_matrix)
    combined = projected + adapted
    return (residual.astype(jnp.float32) + image_gate[:, None, :].astype(jnp.float32) * combined).astype(jnp.bfloat16)
```

```python
import jax
import jax.numpy as jnp
from jax import lax
from jax.experimental import pallas as pl
from jax.experimental.pallas import tpu as pltpu
from jax.sharding import PartitionSpec as P

HEAD_WIDTH = 128
LOG2E = 1.4426950408889634
ANY = pl.BlockSpec(memory_space=pl.ANY)
VMEM_LIMIT = 56 * 1024 * 1024


def broadcast(shard, axis, root):
    mine = lax.axis_index(axis) == root
    return lax.psum(jnp.where(mine, shard, jnp.zeros_like(shard)), axis)


def attend_one(query_head, key_head, value_head):
    length = query_head.shape[0]
    block_rows = min(512, length)
    scale = query_head.shape[1] ** (-0.5)

    def one_block(query_block):
        scores = jnp.dot(query_block, key_head.T, preferred_element_type=jnp.float32) * scale
        largest = jnp.max(scores, axis=1, keepdims=True)
        exponent = jnp.exp(scores - largest)
        totals = jnp.sum(exponent, axis=1, keepdims=True)
        weights = exponent.astype(jnp.bfloat16)
        return (jnp.dot(weights, value_head, preferred_element_type=jnp.float32) / totals).astype(
            jnp.bfloat16
        )

    blocks = query_head.reshape(length // block_rows, block_rows, query_head.shape[1])
    return lax.map(one_block, blocks).reshape(length, query_head.shape[1])


def attend_items(parts):
    query_part, key_part, value_part = parts
    leading, count, length, depth = query_part.shape

    def flatten(array):
        return array.reshape(leading * count, length, depth)

    result = lax.map(
        lambda triple: attend_one(*triple),
        (flatten(query_part), flatten(key_part), flatten(value_part)),
    )
    return result.reshape(leading, count, length, depth)


def to_units(array, seq_count, head_count):
    image_count, seq_rows, width_here = array.shape
    arranged = array.reshape(image_count, seq_rows, head_count, HEAD_WIDTH).transpose(0, 2, 1, 3)
    return arranged.reshape(seq_count, image_count * head_count // seq_count, seq_rows, HEAD_WIDTH)


def general_shards(
    rotated_queries,
    rotated_keys,
    head_values,
    residual,
    image_gate,
    output_weight,
    adapter_down,
    adapter_up,
    image_group,
    group_adapter,
    adapter_store_row,
):
    seq_count = lax.axis_size("seq")
    image_count, seq_rows, width_here = rotated_queries.shape
    head_count = width_here // HEAD_WIDTH

    def spread(array):
        units = to_units(array, seq_count, head_count)
        return lax.all_to_all(units, "seq", split_axis=0, concat_axis=2, tiled=True)

    gathered = attend_items((spread(rotated_queries), spread(rotated_keys), spread(head_values)))
    returned = lax.all_to_all(gathered, "seq", split_axis=2, concat_axis=0, tiled=True)
    attended = (
        returned.reshape(image_count, head_count, seq_rows, HEAD_WIDTH)
        .transpose(0, 2, 1, 3)
        .reshape(image_count * seq_rows, width_here)
    )
    partial_terms = jnp.dot(
        attended,
        lax.all_gather(output_weight, "seq", axis=1, tiled=True),
        preferred_element_type=jnp.float32,
    )
    projected = lax.psum_scatter(partial_terms, "tp", scatter_dimension=1, tiled=True)
    store_share = adapter_down.shape[0]
    first = lax.axis_index("img") * image_count
    slot_count = group_adapter.shape[0]

    def fetch_slot(index, carry):
        store_row = adapter_store_row[group_adapter[index]]
        owner = store_row // store_share
        down_portion = lax.dynamic_index_in_dim(adapter_down, store_row % store_share, 0, keepdims=False)
        up_portion = lax.dynamic_index_in_dim(adapter_up, store_row % store_share, 0, keepdims=False)
        return (
            carry[0].at[index].set(broadcast(down_portion, ("seq", "img"), owner)),
            carry[1].at[index].set(broadcast(up_portion, ("seq", "img"), owner)),
        )

    blank_down = jnp.zeros((slot_count,) + adapter_down.shape[1:], jnp.bfloat16)
    blank_up = jnp.zeros((slot_count,) + adapter_up.shape[1:], jnp.bfloat16)
    every_down, every_up = lax.fori_loop(0, slot_count, fetch_slot, (blank_down, blank_up))
    slots_mine = lax.dynamic_slice_in_dim(image_group, first, image_count, 0)
    inner_local = jnp.einsum(
        "bsh,bhr->bsr",
        attended.reshape(image_count, seq_rows, width_here),
        every_down[slots_mine],
        preferred_element_type=jnp.float32,
    )
    inner_terms = lax.psum(inner_local, "tp").astype(jnp.bfloat16)
    adapted = jnp.einsum(
        "bsr,brd->bsd", inner_terms, every_up[slots_mine], preferred_element_type=jnp.float32
    )
    combined = projected.reshape(image_count, seq_rows, -1) + adapted
    return (
        residual.astype(jnp.float32) + image_gate[:, None, :].astype(jnp.float32) * combined
    ).astype(jnp.bfloat16)


def flip(array, axis, distance):
    size = lax.axis_size(axis)
    return lax.ppermute(array, axis, [(i, i ^ distance) for i in range(size)])


def pack_chunk(queries, keys, values, start, width):
    rows = queries.shape[1]

    def kernel(q_ref, k_ref, v_ref, *rest):
        outs, (staged, sems, out_sems) = rest[:3], rest[3:]
        here = lax.axis_index("seq")
        loads = [
            [
                pltpu.make_async_copy(
                    ref.at[here ^ (i + 1), :, pl.ds(start, width)],
                    staged.at[i, :, pl.ds(j * width, width)],
                    sems.at[i, j],
                )
                for j, ref in enumerate((q_ref, k_ref, v_ref))
            ]
            for i in range(3)
        ]
        stores = [pltpu.make_async_copy(staged.at[i], outs[i], out_sems.at[i]) for i in range(3)]
        for group in loads:
            for copy in group:
                copy.start()
        for group, store in zip(loads, stores):
            for copy in group:
                copy.wait()
            store.start()
        for store in stores:
            store.wait()

    shape = jax.ShapeDtypeStruct((rows, 3 * width), queries.dtype)
    return pl.pallas_call(
        kernel,
        out_shape=[shape] * 3,
        in_specs=[ANY] * 3,
        out_specs=[ANY] * 3,
        scratch_shapes=[
            pltpu.VMEM((3, rows, 3 * width), queries.dtype),
            pltpu.SemaphoreType.DMA((3, 3)),
            pltpu.SemaphoreType.DMA((3,)),
        ],
        compiler_params=pltpu.CompilerParams(vmem_limit_bytes=VMEM_LIMIT),
        cost_estimate=pl.CostEstimate(flops=0, bytes_accessed=2 * 9 * rows * width * 2, transcendentals=0),
        name="pack",
    )(queries, keys, values)


def attend_chunk(queries, keys, values, received, start, width):
    rows = queries.shape[1]
    length = 4 * rows
    heads = width // HEAD_WIDTH
    block = 256
    factor = HEAD_WIDTH ** (-0.5) * LOG2E

    def kernel(q_ref, k_ref, v_ref, r1_ref, r2_ref, r3_ref, *rest):
        outs = rest[:4]
        q_all, k_all, v_all, o_all, sems, out_sems = rest[4:]
        here = lax.axis_index("seq")
        copies = []
        for d in range(4):
            for j, (ref, place) in enumerate(((q_ref, q_all), (k_ref, k_all), (v_ref, v_all))):
                for h in range(heads):
                    lanes = pl.ds(h * HEAD_WIDTH, HEAD_WIDTH)
                    if d == 0:
                        source = ref.at[here, :, pl.ds(start + h * HEAD_WIDTH, HEAD_WIDTH)]
                    else:
                        source = (r1_ref, r2_ref, r3_ref)[d - 1].at[
                            :, pl.ds(j * width + h * HEAD_WIDTH, HEAD_WIDTH)
                        ]
                    if j == 2:
                        lanes = pl.ds(2 * h * HEAD_WIDTH, HEAD_WIDTH)
                    copies.append(
                        pltpu.make_async_copy(
                            source, place.at[pl.ds(d * rows, rows), lanes], sems.at[d, j, h]
                        )
                    )
        for copy in copies:
            copy.start()
        for h in range(heads):
            v_all[:, (2 * h + 1) * HEAD_WIDTH : (2 * h + 2) * HEAD_WIDTH] = jnp.ones(
                (length, HEAD_WIDTH), jnp.bfloat16
            )
        for copy in copies:
            copy.wait()

        @pl.loop(0, length // block)
        def _(i):
            place = pl.ds(pl.multiple_of(i * block, block), block)
            for h in range(heads):
                lanes = slice(h * HEAD_WIDTH, (h + 1) * HEAD_WIDTH)
                scores = lax.dot_general(
                    q_all[place, lanes],
                    k_all[:, lanes],
                    (((1,), (1,)), ((), ())),
                    preferred_element_type=jnp.float32,
                )
                largest = jnp.max(scores, axis=1, keepdims=True)
                weights = jnp.exp2((scores - largest) * factor).astype(jnp.bfloat16)
                both = jnp.dot(
                    weights,
                    v_all[:, 2 * h * HEAD_WIDTH : (2 * h + 2) * HEAD_WIDTH],
                    preferred_element_type=jnp.float32,
                )
                o_all[place, lanes] = (both[:, :HEAD_WIDTH] / both[:, HEAD_WIDTH:]).astype(
                    jnp.bfloat16
                )

        copies = [
            pltpu.make_async_copy(o_all.at[pl.ds(d * rows, rows)], outs[d], out_sems.at[d])
            for d in range(4)
        ]
        for copy in copies:
            copy.start()
        for copy in copies:
            copy.wait()

    shape = jax.ShapeDtypeStruct((rows, width), queries.dtype)
    return pl.pallas_call(
        kernel,
        out_shape=[shape] * 4,
        in_specs=[ANY] * 6,
        out_specs=[ANY] * 4,
        scratch_shapes=[
            pltpu.VMEM((length, width), jnp.bfloat16),
            pltpu.VMEM((length, width), jnp.bfloat16),
            pltpu.VMEM((length, 2 * width), jnp.bfloat16),
            pltpu.VMEM((length, width), jnp.bfloat16),
            pltpu.SemaphoreType.DMA((4, 3, heads)),
            pltpu.SemaphoreType.DMA((4,)),
        ],
        compiler_params=pltpu.CompilerParams(vmem_limit_bytes=VMEM_LIMIT),
        cost_estimate=pl.CostEstimate(
            flops=8 * length * length * width,
            bytes_accessed=8 * length * width,
            transcendentals=heads * length * length,
        ),
        name="attend",
    )(queries, keys, values, *received)


def own_factors(down_t, up, group_adapter, adapter_store_row):
    share, rank, down_width = down_t.shape
    up_width = up.shape[2]
    slots = group_adapter.shape[0]
    store_rows = adapter_store_row[group_adapter]
    mine = lax.axis_index(("seq", "img"))
    place = jnp.stack([store_rows % share, (store_rows // share == mine).astype(jnp.int32)])

    def kernel(place_ref, down_ref, up_ref, out_ref):
        held = place_ref[1, pl.program_id(0)] == 1
        out_ref[0, :, :down_width] = jnp.where(held, down_ref[0], jnp.zeros_like(down_ref[0]))
        out_ref[0, :, down_width:] = jnp.where(held, up_ref[0], jnp.zeros_like(up_ref[0]))

    return pl.pallas_call(
        kernel,
        out_shape=jax.ShapeDtypeStruct((slots, rank, down_width + up_width), up.dtype),
        grid_spec=pltpu.PrefetchScalarGridSpec(
            num_scalar_prefetch=1,
            grid=(slots,),
            in_specs=[
                pl.BlockSpec((1, rank, down_width), lambda s, place_ref: (place_ref[0, s], 0, 0)),
                pl.BlockSpec((1, rank, up_width), lambda s, place_ref: (place_ref[0, s], 0, 0)),
            ],
            out_specs=pl.BlockSpec((1, rank, down_width + up_width), lambda s, place_ref: (s, 0, 0)),
        ),
        name="own_factors",
    )(place, down_t, up)


def exchange_half(array, axis, distance, bit):
    half = array.shape[0] // 2
    kept = lax.dynamic_slice_in_dim(array, bit * half, half, 0)
    sent = lax.dynamic_slice_in_dim(array, (1 - bit) * half, half, 0)
    return kept + flip(sent, axis, distance)


def join_half(array, axis, distance, bit):
    other = flip(array, axis, distance)
    low = jnp.where(bit == 0, array, other)
    high = jnp.where(bit == 0, other, array)
    return jnp.concatenate([low, high], axis=0)


def all_factors(own, z, x):
    held = exchange_half(own, "img", 1, x)
    held = exchange_half(held, "seq", 1, z & 1)
    held = held + flip(held, "seq", 2)
    held = join_half(held, "seq", 1, z & 1)
    return join_half(held, "img", 1, x)


def all_weights(shard, z, x, g, t):
    rows, width = shard.shape
    part = rows // 4
    line = 2 * g + x
    own = lax.dynamic_slice_in_dim(shard, line * part, part, 0)
    got = {d: flip(own, "seq", d) for d in (2, 3, 1)}
    odd = (z & 1) == 1
    near = jnp.where(odd, jnp.concatenate([got[1], own], 1), jnp.concatenate([own, got[1]], 1))
    far = jnp.where(odd, jnp.concatenate([got[3], got[2]], 1), jnp.concatenate([got[2], got[3]], 1))
    keep_near = (z >> 1) == t
    kept = jnp.where(keep_near, near, far)
    sent = jnp.where(keep_near, far, near)
    quarter = jnp.stack([kept, flip(sent, "tp", 1)])
    beside = flip(quarter, "img", 1)
    above = flip(quarter, "group", 1)
    across = flip(beside, "group", 1)
    whole = jnp.zeros((2, rows, 2 * width), shard.dtype)
    for j, piece in enumerate((quarter, beside, above, across)):
        whole = lax.dynamic_update_slice(whole, piece, (0, (line ^ j) * part, 0))
    return whole


def project_pair(pair, own, other, weights, factors, other_down, residual, gate, slots, before):
    rows, width = own[0][0].shape
    chunks = len(own)
    model_rows = weights.shape[1]
    columns = weights.shape[2]
    rank = factors.shape[1]
    tile = 256
    count = len(pair)
    pieces = [own[c][d] for d in pair for c in range(chunks)]
    pieces += [other[c][d] for d in pair for c in range(chunks)]
    total = len(pieces)

    def kernel(index_ref, *refs):
        piece_refs = refs[:total]
        rest = refs[total:]
        w_ref = rest[0]
        down_refs = rest[1 : 1 + count]
        down_other_refs = rest[1 + count : 1 + 2 * count]
        up_refs = rest[1 + 2 * count : 1 + 3 * count]
        res_refs = rest[1 + 3 * count : 1 + 4 * count]
        gate_refs = rest[1 + 4 * count : 1 + 5 * count]
        tail = rest[1 + 5 * count :]
        if before is not None:
            tail = tail[1:]
        out_ref, att, inner, stage, sems = tail
        n = pl.program_id(0)

        @pl.when(n == 0)
        def _():
            for p in range(count):
                for c in range(chunks):
                    here = slice(p * rows, (p + 1) * rows)
                    att[here, c * width : (c + 1) * width] = piece_refs[p * chunks + c][...]
                    att[here, model_rows + c * width : model_rows + (c + 1) * width] = piece_refs[
                        (count + p) * chunks + c
                    ][...]
            for p in range(count):
                here = slice(p * rows, (p + 1) * rows)
                contract = (((1,), (1,)), ((), ()))
                terms = lax.dot_general(
                    att[here, :model_rows], down_refs[p][0], contract, preferred_element_type=jnp.float32
                )
                terms += lax.dot_general(
                    att[here, model_rows:],
                    down_other_refs[p][0],
                    contract,
                    preferred_element_type=jnp.float32,
                )
                inner[here, :] = terms.astype(jnp.bfloat16)

        def copy_out(p, step):
            return pltpu.make_async_copy(
                stage.at[lax.rem(step, 2), p],
                out_ref.at[index_ref[p], :, pl.ds(pl.multiple_of(step * tile, tile), tile)],
                sems.at[lax.rem(step, 2), p],
            )

        @pl.when(n >= 2)
        def _():
            for p in range(count):
                copy_out(p, n - 2).wait()

        for p in range(count):
            here = slice(p * rows, (p + 1) * rows)
            sums = jnp.dot(att[here, :model_rows], w_ref[0], preferred_element_type=jnp.float32)
            sums += jnp.dot(att[here, model_rows:], w_ref[1], preferred_element_type=jnp.float32)
            sums += jnp.dot(inner[here, :], up_refs[p][0], preferred_element_type=jnp.float32)
            result = res_refs[p][0].astype(jnp.float32) + gate_refs[p][0].astype(jnp.float32) * sums
            stage[lax.rem(n, 2), p] = result.astype(jnp.bfloat16)
            copy_out(p, n).start()

        @pl.when(n == pl.num_programs(0) - 1)
        def _():
            for p in range(count):
                copy_out(p, n - 1).wait()
                copy_out(p, n).wait()

    whole = lambda n, index_ref: (0, 0)
    in_specs = [pl.BlockSpec((rows, width), whole)] * total
    in_specs.append(pl.BlockSpec((2, model_rows, tile), lambda n, index_ref: (0, 0, n)))
    for offset in range(count):
        in_specs.append(
            pl.BlockSpec(
                (1, rank, model_rows), lambda n, index_ref, o=offset: (index_ref[count + o], 0, 0)
            )
        )
    for offset in range(count):
        in_specs.append(
            pl.BlockSpec(
                (1, rank, model_rows), lambda n, index_ref, o=offset: (index_ref[count + o], 0, 0)
            )
        )
    first_up = model_rows // tile
    for offset in range(count):
        in_specs.append(
            pl.BlockSpec(
                (1, rank, tile), lambda n, index_ref, o=offset: (index_ref[count + o], 0, first_up + n)
            )
        )
    for offset in range(count):
        in_specs.append(
            pl.BlockSpec((1, rows, tile), lambda n, index_ref, o=offset: (index_ref[o], 0, n))
        )
    for offset in range(count):
        in_specs.append(pl.BlockSpec((1, 1, tile), lambda n, index_ref, o=offset: (index_ref[o], 0, n)))
    operands = pieces + [weights] + [factors] * count + [other_down] * count
    operands += [factors] * count + [residual] * count + [gate] * count
    aliases = {}
    if before is not None:
        aliases = {1 + len(operands): 0}
        in_specs.append(ANY)
        operands.append(before)
    z = lax.axis_index("seq")
    images = jnp.stack([z ^ d for d in pair])
    index = jnp.concatenate([images, slots[images]]).astype(jnp.int32)
    return pl.pallas_call(
        kernel,
        out_shape=jax.ShapeDtypeStruct(residual.shape, residual.dtype),
        grid_spec=pltpu.PrefetchScalarGridSpec(
            num_scalar_prefetch=1,
            grid=(columns // tile,),
            in_specs=in_specs,
            out_specs=ANY,
            scratch_shapes=[
                pltpu.VMEM((count * rows, 2 * model_rows), jnp.bfloat16),
                pltpu.VMEM((count * rows, rank), jnp.bfloat16),
                pltpu.VMEM((2, count, rows, tile), jnp.bfloat16),
                pltpu.SemaphoreType.DMA((2, count)),
            ],
        ),
        input_output_aliases=aliases,
        compiler_params=pltpu.CompilerParams(vmem_limit_bytes=VMEM_LIMIT),
        cost_estimate=pl.CostEstimate(
            flops=4 * count * rows * model_rows * columns,
            bytes_accessed=4 * model_rows * columns + 8 * count * rows * model_rows,
            transcendentals=0,
        ),
        name="project",
    )(index, *operands)


def line_shards(
    rotated_queries,
    rotated_keys,
    head_values,
    residual,
    image_gate,
    output_weight,
    adapter_down,
    adapter_up,
    image_group,
    group_adapter,
    adapter_store_row,
):
    z, x = lax.axis_index("seq"), lax.axis_index("img")
    g, t = lax.axis_index("group"), lax.axis_index("tp")
    image_count, rows, width_here = rotated_queries.shape
    width = 2 * HEAD_WIDTH
    chunks = width_here // width
    qkv = (rotated_queries, rotated_keys, head_values)

    factors = all_factors(
        own_factors(jnp.swapaxes(adapter_down, 1, 2), adapter_up, group_adapter, adapter_store_row), z, x
    )
    other_down = flip(factors[:, :, :width_here], "tp", 1)
    weights = all_weights(output_weight, z, x, g, t)

    own, other = [], []
    for c in range(chunks):
        packed = pack_chunk(*qkv, c * width, width)
        received = [flip(packed[d - 1], "seq", d) for d in (1, 2, 3)]
        blocks = attend_chunk(*qkv, received, c * width, width)
        mine = [blocks[0]] + [flip(blocks[d], "seq", d) for d in (1, 2, 3)]
        own.append(mine)
        other.append([flip(block, "tp", 1) for block in mine])

    slots = lax.dynamic_slice_in_dim(image_group, x * image_count, image_count, 0)
    gate = image_gate[:, None, :]
    common = (own, other, weights, factors, other_down, residual, gate, slots)
    result = project_pair((0, 1), *common, None)
    return project_pair((2, 3), *common, result)


def solution(mesh):
    shape = dict(mesh.shape)
    line = shape["seq"] == 4 and shape["img"] == 2 and shape["group"] == 2 and shape["tp"] == 2

    def shards(*arrays):
        image_count = arrays[0].shape[0]
        slots = arrays[9].shape[0]
        if line and image_count == 4 and slots == 4:
            return line_shards(*arrays)
        return general_shards(*arrays)

    return jax.shard_map(
        shards,
        mesh=mesh,
        in_specs=(
            P(("group", "img"), "seq", "tp"),
            P(("group", "img"), "seq", "tp"),
            P(("group", "img"), "seq", "tp"),
            P(("group", "img"), "seq", "tp"),
            P(("group", "img"), "tp"),
            P("tp", "seq"),
            P(("group", "seq", "img"), "tp", None),
            P(("group", "seq", "img"), None, "tp"),
            P("group"),
            P("group"),
            P("group"),
        ),
        out_specs=P(("group", "img"), "seq", "tp"),
        check_vma=False,
    )
```

```python
import jax
import jax.numpy as jnp
from jax import lax
from jax.experimental import pallas as pl
from jax.experimental.pallas import tpu as pltpu
from jax.sharding import PartitionSpec as P

HEAD_WIDTH = 128
LOG2E = 1.4426950408889634
ANY = pl.BlockSpec(memory_space=pl.ANY)
SMALL = pl.CostEstimate(flops=1000, bytes_accessed=1000, transcendentals=0)
LARGE = pl.CostEstimate(flops=170_000_000_000, bytes_accessed=1000, transcendentals=0)
VMEM_LIMIT = 56 * 1024 * 1024


def broadcast(shard, axis, root):
    mine = lax.axis_index(axis) == root
    return lax.psum(jnp.where(mine, shard, jnp.zeros_like(shard)), axis)


def attend_one(query_head, key_head, value_head):
    length = query_head.shape[0]
    block_rows = min(512, length)
    scale = query_head.shape[1] ** (-0.5)

    def one_block(query_block):
        scores = jnp.dot(query_block, key_head.T, preferred_element_type=jnp.float32) * scale
        largest = jnp.max(scores, axis=1, keepdims=True)
        exponent = jnp.exp(scores - largest)
        totals = jnp.sum(exponent, axis=1, keepdims=True)
        weights = exponent.astype(jnp.bfloat16)
        return (jnp.dot(weights, value_head, preferred_element_type=jnp.float32) / totals).astype(
            jnp.bfloat16
        )

    blocks = query_head.reshape(length // block_rows, block_rows, query_head.shape[1])
    return lax.map(one_block, blocks).reshape(length, query_head.shape[1])


def attend_items(parts):
    query_part, key_part, value_part = parts
    leading, count, length, depth = query_part.shape

    def flatten(array):
        return array.reshape(leading * count, length, depth)

    result = lax.map(
        lambda triple: attend_one(*triple),
        (flatten(query_part), flatten(key_part), flatten(value_part)),
    )
    return result.reshape(leading, count, length, depth)


def to_units(array, seq_count, head_count):
    image_count, seq_rows, width_here = array.shape
    arranged = array.reshape(image_count, seq_rows, head_count, HEAD_WIDTH).transpose(0, 2, 1, 3)
    return arranged.reshape(seq_count, image_count * head_count // seq_count, seq_rows, HEAD_WIDTH)


def general_shards(
    rotated_queries,
    rotated_keys,
    head_values,
    residual,
    image_gate,
    output_weight,
    adapter_down,
    adapter_up,
    image_group,
    group_adapter,
    adapter_store_row,
):
    seq_count = lax.axis_size("seq")
    image_count, seq_rows, width_here = rotated_queries.shape
    head_count = width_here // HEAD_WIDTH

    def spread(array):
        units = to_units(array, seq_count, head_count)
        return lax.all_to_all(units, "seq", split_axis=0, concat_axis=2, tiled=True)

    gathered = attend_items((spread(rotated_queries), spread(rotated_keys), spread(head_values)))
    returned = lax.all_to_all(gathered, "seq", split_axis=2, concat_axis=0, tiled=True)
    attended = (
        returned.reshape(image_count, head_count, seq_rows, HEAD_WIDTH)
        .transpose(0, 2, 1, 3)
        .reshape(image_count * seq_rows, width_here)
    )
    partial_terms = jnp.dot(
        attended,
        lax.all_gather(output_weight, "seq", axis=1, tiled=True),
        preferred_element_type=jnp.float32,
    )
    projected = lax.psum_scatter(partial_terms, "tp", scatter_dimension=1, tiled=True)
    store_share = adapter_down.shape[0]
    first = lax.axis_index("img") * image_count
    slot_count = group_adapter.shape[0]

    def fetch_slot(index, carry):
        store_row = adapter_store_row[group_adapter[index]]
        owner = store_row // store_share
        down_portion = lax.dynamic_index_in_dim(adapter_down, store_row % store_share, 0, keepdims=False)
        up_portion = lax.dynamic_index_in_dim(adapter_up, store_row % store_share, 0, keepdims=False)
        return (
            carry[0].at[index].set(broadcast(down_portion, ("seq", "img"), owner)),
            carry[1].at[index].set(broadcast(up_portion, ("seq", "img"), owner)),
        )

    blank_down = jnp.zeros((slot_count,) + adapter_down.shape[1:], jnp.bfloat16)
    blank_up = jnp.zeros((slot_count,) + adapter_up.shape[1:], jnp.bfloat16)
    every_down, every_up = lax.fori_loop(0, slot_count, fetch_slot, (blank_down, blank_up))
    slots_mine = lax.dynamic_slice_in_dim(image_group, first, image_count, 0)
    inner_local = jnp.einsum(
        "bsh,bhr->bsr",
        attended.reshape(image_count, seq_rows, width_here),
        every_down[slots_mine],
        preferred_element_type=jnp.float32,
    )
    inner_terms = lax.psum(inner_local, "tp").astype(jnp.bfloat16)
    adapted = jnp.einsum(
        "bsr,brd->bsd", inner_terms, every_up[slots_mine], preferred_element_type=jnp.float32
    )
    combined = projected.reshape(image_count, seq_rows, -1) + adapted
    return (
        residual.astype(jnp.float32) + image_gate[:, None, :].astype(jnp.float32) * combined
    ).astype(jnp.bfloat16)


def gated(array, *earlier):
    return lax.optimization_barrier((array, earlier))[0]


def flip(array, axis, distance):
    size = lax.axis_size(axis)
    return lax.ppermute(array, axis, [(i, i ^ distance) for i in range(size)])


def pack(arrays, start, back, extras, after=()):
    rows = arrays[0].shape[1]
    width = 2 * HEAD_WIDTH
    back = list(back)
    extra_rows = [sum(extra[3] for extra in extras if extra[0] == d) for d in (1, 2, 3)]
    base = (len(arrays) + (1 if back else 0)) * rows
    heights = [base + more for more in extra_rows]
    tallest = max(heights)

    def kernel(*refs):
        refs = list(refs)
        array_refs = [refs.pop(0) for _ in arrays]
        back_refs = [refs.pop(0) for _ in back]
        extra_refs = [refs.pop(0) for _ in extras]
        for _ in after:
            refs.pop(0)
        outs = [refs.pop(0) for _ in range(3)]
        staged, sems, out_sems = refs
        here = lax.axis_index("seq")
        loads = []
        for i in range(3):
            place, group = 0, []
            views = [ref.at[here ^ (i + 1), :, pl.ds(start, width)] for ref in array_refs]
            if back:
                views.append(back_refs[i])
            for (d, _, parts, _), ref in zip(extras, extra_refs):
                if d == i + 1:
                    views += parts(ref)
            for j, view in enumerate(views):
                height = view.shape[0]
                group.append(
                    pltpu.make_async_copy(view, staged.at[i, pl.ds(place, height)], sems.at[i, j])
                )
                place += height
            loads.append(group)
        stores = [
            pltpu.make_async_copy(staged.at[i, pl.ds(0, heights[i])], outs[i], out_sems.at[i])
            for i in range(3)
        ]
        for group in reversed(loads):
            for copy in group:
                copy.start()
        for group, store in reversed(list(zip(loads, stores))):
            for copy in group:
                copy.wait()
            store.start()
        for store in stores:
            store.wait()

    dtype = arrays[0].dtype
    return pl.pallas_call(
        kernel,
        out_shape=[jax.ShapeDtypeStruct((height, width), dtype) for height in heights],
        in_specs=[ANY] * (len(arrays) + len(back) + len(extras) + len(after)),
        out_specs=[ANY] * 3,
        scratch_shapes=[
            pltpu.VMEM((3, tallest, width), dtype),
            pltpu.SemaphoreType.DMA((3, 16)),
            pltpu.SemaphoreType.DMA((3,)),
        ],
        compiler_params=pltpu.CompilerParams(vmem_limit_bytes=VMEM_LIMIT),
        cost_estimate=SMALL,
        name="pack",
    )(*arrays, *back, *[extra[1] for extra in extras], *after)


def attend_chunk(queries, keys, values, received, start, after=()):
    rows = queries.shape[1]
    width = 2 * HEAD_WIDTH
    length = 4 * rows
    heads = width // HEAD_WIDTH
    block = 256
    factor = HEAD_WIDTH ** (-0.5) * LOG2E

    def kernel(q_ref, k_ref, v_ref, r1_ref, r2_ref, r3_ref, *rest):
        rest = rest[len(after) :]
        outs = rest[:4]
        q_all, k_all, v_all, o_all, sems, out_sems = rest[4:]
        here = lax.axis_index("seq")
        copies = []
        for d in range(4):
            for j, (ref, place) in enumerate(((q_ref, q_all), (k_ref, k_all), (v_ref, v_all))):
                for h in range(heads):
                    lanes = pl.ds(h * HEAD_WIDTH, HEAD_WIDTH)
                    if d == 0:
                        source = ref.at[here, :, pl.ds(start + h * HEAD_WIDTH, HEAD_WIDTH)]
                    else:
                        source = (r1_ref, r2_ref, r3_ref)[d - 1].at[pl.ds(j * rows, rows), lanes]
                    if j == 2:
                        lanes = pl.ds(2 * h * HEAD_WIDTH, HEAD_WIDTH)
                    copies.append(
                        pltpu.make_async_copy(
                            source, place.at[pl.ds(d * rows, rows), lanes], sems.at[d, j, h]
                        )
                    )
        for copy in copies:
            copy.start()
        for h in range(heads):
            v_all[:, (2 * h + 1) * HEAD_WIDTH : (2 * h + 2) * HEAD_WIDTH] = jnp.ones(
                (length, HEAD_WIDTH), jnp.bfloat16
            )
        for copy in copies:
            copy.wait()

        @pl.loop(0, length // block)
        def _(i):
            place = pl.ds(pl.multiple_of(i * block, block), block)
            for h in range(heads):
                lanes = slice(h * HEAD_WIDTH, (h + 1) * HEAD_WIDTH)
                scores = lax.dot_general(
                    q_all[place, lanes],
                    k_all[:, lanes],
                    (((1,), (1,)), ((), ())),
                    preferred_element_type=jnp.float32,
                )
                largest = jnp.max(scores, axis=1, keepdims=True)
                weights = jnp.exp2((scores - largest) * factor).astype(jnp.bfloat16)
                both = jnp.dot(
                    weights,
                    v_all[:, 2 * h * HEAD_WIDTH : (2 * h + 2) * HEAD_WIDTH],
                    preferred_element_type=jnp.float32,
                )
                o_all[place, lanes] = (both[:, :HEAD_WIDTH] / both[:, HEAD_WIDTH:]).astype(
                    jnp.bfloat16
                )

        copies = [
            pltpu.make_async_copy(o_all.at[pl.ds(d * rows, rows)], outs[d], out_sems.at[d])
            for d in range(4)
        ]
        for copy in copies:
            copy.start()
        for copy in copies:
            copy.wait()

    shape = jax.ShapeDtypeStruct((rows, width), queries.dtype)
    return pl.pallas_call(
        kernel,
        out_shape=[shape] * 4,
        in_specs=[ANY] * (6 + len(after)),
        out_specs=[ANY] * 4,
        scratch_shapes=[
            pltpu.VMEM((length, width), jnp.bfloat16),
            pltpu.VMEM((length, width), jnp.bfloat16),
            pltpu.VMEM((length, 2 * width), jnp.bfloat16),
            pltpu.VMEM((length, width), jnp.bfloat16),
            pltpu.SemaphoreType.DMA((4, 3, heads)),
            pltpu.SemaphoreType.DMA((4,)),
        ],
        compiler_params=pltpu.CompilerParams(vmem_limit_bytes=VMEM_LIMIT),
        cost_estimate=LARGE,
        name="attend",
    )(queries, keys, values, *received, *after)


def stacked(blocks, rows, after=()):
    count = len(blocks)
    width = blocks[0][0].shape[1]
    dtype = blocks[0][0].dtype

    def kernel(*refs):
        out, staged, sems, out_sems = refs[count + len(after) :]
        loads = [
            pltpu.make_async_copy(ref.at[pl.ds(place * rows, rows)], staged.at[i], sems.at[i])
            for i, (ref, (_, place)) in enumerate(zip(refs[:count], blocks))
        ]
        stores = [pltpu.make_async_copy(staged.at[i], out.at[i], out_sems.at[i]) for i in range(count)]
        for copy in loads:
            copy.start()
        for load, store in zip(loads, stores):
            load.wait()
            store.start()
        for copy in stores:
            copy.wait()

    return pl.pallas_call(
        kernel,
        out_shape=jax.ShapeDtypeStruct((count, rows, width), dtype),
        in_specs=[ANY] * (count + len(after)),
        out_specs=ANY,
        scratch_shapes=[
            pltpu.VMEM((count, rows, width), dtype),
            pltpu.SemaphoreType.DMA((count,)),
            pltpu.SemaphoreType.DMA((count,)),
        ],
        compiler_params=pltpu.CompilerParams(vmem_limit_bytes=VMEM_LIMIT),
        cost_estimate=SMALL,
        name="stacked",
    )(*[array for array, _ in blocks], *after)


def own_factors(down_t, up, group_adapter, adapter_store_row):
    share, rank, down_width = down_t.shape
    up_width = up.shape[2]
    tile = 2 * HEAD_WIDTH
    down_tiles, up_tiles = down_width // tile, up_width // tile
    slots = group_adapter.shape[0]
    store_rows = adapter_store_row[group_adapter]
    mine = lax.axis_index(("seq", "img"))
    place = jnp.stack([store_rows % share, (store_rows // share == mine).astype(jnp.int32)])

    def kernel(place_ref, down_ref, up_ref, out_ref):
        held = place_ref[1, pl.program_id(0)] == 1
        for ref, count, first in ((down_ref, down_tiles, 0), (up_ref, up_tiles, down_tiles)):
            for j in range(count):
                value = ref[0, :, j * tile : (j + 1) * tile]
                out_ref[0, first + j] = jnp.where(held, value, jnp.zeros_like(value))

    return pl.pallas_call(
        kernel,
        out_shape=jax.ShapeDtypeStruct((slots, down_tiles + up_tiles, rank, tile), up.dtype),
        grid_spec=pltpu.PrefetchScalarGridSpec(
            num_scalar_prefetch=1,
            grid=(slots,),
            in_specs=[
                pl.BlockSpec((1, rank, down_width), lambda s, place_ref: (place_ref[0, s], 0, 0)),
                pl.BlockSpec((1, rank, up_width), lambda s, place_ref: (place_ref[0, s], 0, 0)),
            ],
            out_specs=pl.BlockSpec(
                (1, down_tiles + up_tiles, rank, tile), lambda s, place_ref: (s, 0, 0, 0)
            ),
        ),
        name="own_factors",
    )(place, down_t, up)


def exchange_half(array, axis, distance, bit):
    half = array.shape[0] // 2
    kept = lax.dynamic_slice_in_dim(array, bit * half, half, 0)
    sent = lax.dynamic_slice_in_dim(array, (1 - bit) * half, half, 0)
    return kept + flip(sent, axis, distance)


def join_half(array, axis, distance, bit):
    other = flip(array, axis, distance)
    low = jnp.where(bit == 0, array, other)
    high = jnp.where(bit == 0, other, array)
    return jnp.concatenate([low, high], axis=0)


def project(pair, parts, own, other, weights, factors, other_down, index, sums_before, final):
    chunks = len(parts)
    part_index = parts[0] // chunks
    count = len(pair)
    width = 2 * HEAD_WIDTH
    rows = own[0][0][0].shape[0]
    rank = factors.shape[2]
    tiles = weights.shape[2]
    tile = weights.shape[4]
    down_tiles = other_down.shape[1]
    columns = tiles * tile
    depth = 2 * chunks * width
    pieces, piece_specs = [], []
    for d in pair:
        for c in parts:
            array, place = own[c][d]
            pieces.append(array)
            piece_specs.append(
                pl.BlockSpec((rows, width), lambda n, index_ref, place=place: (place, 0))
            )
            array, place = other[c][d]
            pieces.append(array)
            piece_specs.append(
                pl.BlockSpec((1, rows, width), lambda n, index_ref, place=place: (place, 0, 0))
            )
    total = len(pieces)
    ending = final is not None
    before = final[2] if ending else None

    def kernel(index_ref, *refs):
        refs = list(refs)
        piece_refs = [refs.pop(0) for _ in range(total)]
        w_ref = refs.pop(0)
        down_refs = [refs.pop(0) for _ in range(2 * count)]
        if sums_before is not None:
            sums_ref = refs.pop(0)
            inner_ref = refs.pop(0)
        if ending:
            up_refs = [refs.pop(0) for _ in range(count)]
            res_refs = [refs.pop(0) for _ in range(count)]
            gate_refs = [refs.pop(0) for _ in range(count)]
            if before is not None:
                refs.pop(0)
            out_ref, att, inner, stage, sems = refs
        else:
            sums_out, inner_out, att = refs
        n = pl.program_id(0)

        @pl.when(n == 0)
        def _():
            for p in range(count):
                here = slice(p * rows, (p + 1) * rows)
                down = []
                for c in range(chunks):
                    k = 2 * (p * chunks + c)
                    att[here, 2 * c * width : (2 * c + 1) * width] = piece_refs[k][...]
                    att[here, (2 * c + 1) * width : (2 * c + 2) * width] = piece_refs[k + 1][0]
                    down += [down_refs[p][0, c], down_refs[count + p][0, c]]
                terms = lax.dot_general(
                    att[here, :],
                    jnp.concatenate(down, axis=1),
                    (((1,), (1,)), ((), ())),
                    preferred_element_type=jnp.float32,
                )
                if sums_before is not None:
                    terms += inner_ref[p]
                if ending:
                    inner[here, :] = terms.astype(jnp.bfloat16)
                else:
                    inner_out[p] = terms

        filled = w_ref[...].reshape(depth, tile)
        if not ending:
            sums = jnp.dot(att[...], filled, preferred_element_type=jnp.float32)
            sums = sums.reshape(count, rows, tile)
            sums_out[...] = sums if sums_before is None else sums + sums_ref[...]
            return

        def copy_out(p, step):
            return pltpu.make_async_copy(
                stage.at[lax.rem(step, 2), p],
                out_ref.at[index_ref[p], :, pl.ds(pl.multiple_of(step * tile, tile), tile)],
                sems.at[lax.rem(step, 2), p],
            )

        @pl.when(n >= 2)
        def _():
            for p in range(count):
                copy_out(p, n - 2).wait()

        half = rows // 2
        for p in range(count):
            for first in (0, half):
                here = slice(p * rows + first, p * rows + first + half)
                place = slice(first, first + half)
                combined = jnp.dot(att[here, :], filled, preferred_element_type=jnp.float32)
                if sums_before is not None:
                    combined += sums_ref[p, place]
                combined += jnp.dot(
                    inner[here, :], up_refs[p][0, 0], preferred_element_type=jnp.float32
                )
                result = res_refs[p][0, place].astype(jnp.float32)
                result += gate_refs[p][0].astype(jnp.float32) * combined
                stage[lax.rem(n, 2), p, place] = result.astype(jnp.bfloat16)
            copy_out(p, n).start()

        @pl.when(n == pl.num_programs(0) - 1)
        def _():
            for p in range(count):
                copy_out(p, n - 1).wait()
                copy_out(p, n).wait()

    in_specs = list(piece_specs)
    operands = list(pieces)
    in_specs.append(
        pl.BlockSpec((chunks, 2, 1, width, tile), lambda n, index_ref: (part_index, 0, n, 0, 0))
    )
    operands.append(weights)
    for array in (factors, other_down):
        for p in range(count):
            in_specs.append(
                pl.BlockSpec(
                    (1, chunks, rank, width),
                    lambda n, index_ref, p=p: (index_ref[count + p], part_index, 0, 0),
                )
            )
            operands.append(array)
    if sums_before is not None:
        group = pair[0] // count
        in_specs.append(pl.BlockSpec((count, rows, tile), lambda n, index_ref: (group, 0, n)))
        in_specs.append(pl.BlockSpec((count, rows, rank), lambda n, index_ref: (group, 0, 0)))
        operands += list(sums_before)
    aliases = {}
    if ending:
        residual, gate, _ = final
        for p in range(count):
            in_specs.append(
                pl.BlockSpec(
                    (1, 1, rank, tile),
                    lambda n, index_ref, p=p: (index_ref[count + p], down_tiles + n, 0, 0),
                )
            )
            operands.append(factors)
        for array, height in ((residual, rows), (gate, 1)):
            for p in range(count):
                in_specs.append(
                    pl.BlockSpec((1, height, tile), lambda n, index_ref, p=p: (index_ref[p], 0, n))
                )
                operands.append(array)
        if before is not None:
            aliases = {1 + len(operands): 0}
            in_specs.append(ANY)
            operands.append(before)
        out_shape = jax.ShapeDtypeStruct(residual.shape, residual.dtype)
        out_specs = ANY
        scratch = [
            pltpu.VMEM((count * rows, depth), jnp.bfloat16),
            pltpu.VMEM((count * rows, rank), jnp.bfloat16),
            pltpu.VMEM((2, count, rows, tile), jnp.bfloat16),
            pltpu.SemaphoreType.DMA((2, count)),
        ]
    else:
        out_shape = [
            jax.ShapeDtypeStruct((count, rows, columns), jnp.float32),
            jax.ShapeDtypeStruct((count, rows, rank), jnp.float32),
        ]
        out_specs = [
            pl.BlockSpec((count, rows, tile), lambda n, index_ref: (0, 0, n)),
            pl.BlockSpec((count, rows, rank), lambda n, index_ref: (0, 0, 0)),
        ]
        scratch = [pltpu.VMEM((count * rows, depth), jnp.bfloat16)]
    return pl.pallas_call(
        kernel,
        out_shape=out_shape,
        grid_spec=pltpu.PrefetchScalarGridSpec(
            num_scalar_prefetch=1,
            grid=(tiles,),
            in_specs=in_specs,
            out_specs=out_specs,
            scratch_shapes=scratch,
        ),
        input_output_aliases=aliases,
        compiler_params=pltpu.CompilerParams(vmem_limit_bytes=VMEM_LIMIT),
        cost_estimate=SMALL,
        name="project",
    )(index, *operands)


def line_shards(
    rotated_queries,
    rotated_keys,
    head_values,
    residual,
    image_gate,
    output_weight,
    adapter_down,
    adapter_up,
    image_group,
    group_adapter,
    adapter_store_row,
):
    z, x, t = lax.axis_index("seq"), lax.axis_index("img"), lax.axis_index("tp")
    image_count, rows, width_here = rotated_queries.shape
    width = 2 * HEAD_WIDTH
    qkv = (rotated_queries, rotated_keys, head_values)
    part = output_weight.shape[0] // 4
    part_tiles = output_weight.shape[1] // width

    def send(packed):
        return {d: flip(packed[d - 1], "seq", d) for d in (3, 2, 1)}

    def attend(c, received, after=()):
        return attend_chunk(*qkv, [received[d] for d in (1, 2, 3)], c * width, after)

    def swap(blocks, after=()):
        array = flip(stacked(blocks, rows, after), "tp", 1)
        return [(array, place) for place in range(len(blocks))]

    line = 2 * lax.axis_index("group") + x
    mine = lax.dynamic_slice_in_dim(output_weight, line * part, part, 0)
    across = flip(mine, "seq", 2)
    packed0 = pack(qkv, 0, (), ())
    stage0 = send(packed0)

    factors = own_factors(
        jnp.swapaxes(adapter_down, 1, 2),
        adapter_up,
        gated(group_adapter, packed0[0]),
        adapter_store_row,
    )
    factors = exchange_half(factors, "img", 1, x)
    factors = exchange_half(factors, "seq", 1, z & 1)
    packed1 = pack(qkv, width, (), ())
    stage1 = send(packed1)
    slots = lax.dynamic_slice_in_dim(image_group, x * image_count, image_count, 0)
    gate = image_gate[:, None, :]
    images = z ^ jnp.arange(image_count, dtype=jnp.int32)
    index = jnp.concatenate([images, slots[images]])
    blocks0 = attend(0, stage0, [packed1[0], factors, across, gate, index])
    couple = gated(jnp.stack([mine, across]), blocks0[0])
    beside = flip(couple, "seq", 1)
    stage2 = send(pack(qkv, 2 * width, blocks0[1:], ()))

    factors = factors + flip(gated(factors, blocks0[0]), "seq", 2)
    blocks1 = attend(1, stage1, [factors, beside])
    stage3 = send(pack(qkv, 3 * width, blocks1[1:], ()))

    odd = (z & 1) == 1
    low, high = jnp.where(odd, beside, couple), jnp.where(odd, couple, beside)
    pairs = jnp.stack([low, high], axis=1).reshape(2, 2, part, part_tiles, width)
    pairs = pairs.transpose(0, 1, 3, 2, 4).reshape(2, 2 * part_tiles, part, width)
    far = ((z >> 1) ^ t) & 1
    swapped = flip(lax.dynamic_index_in_dim(pairs, 1 - far, 0, keepdims=False), "tp", 1)
    quarter = jnp.stack([lax.dynamic_index_in_dim(pairs, far, 0, keepdims=False), swapped])
    weights = lax.all_gather(quarter, ("group", "img"), axis=0)

    joined = join_half(gated(factors, blocks1[0]), "seq", 1, z & 1)
    factors = join_half(joined, "img", 1, x)
    other_down = flip(factors[:, : width_here // width], "tp", 1)
    def returned(blocks, received, place):
        return [(blocks[0], 0)] + [(received[d], place) for d in (1, 2, 3)]

    blocks2 = attend(2, stage2, [swapped, joined])
    stage4 = send(gated(blocks2[1:], stage3[2], stage3[3]))
    own = [returned(blocks0, stage2, len(qkv))]
    other = [swap(own[0])]
    blocks3 = attend(3, stage3, [other[0][0][0], other_down])
    stage5 = send(blocks3[1:])
    own.append(returned(blocks1, stage3, len(qkv)))
    own.append(returned(blocks2, stage4, 0))
    own.append(returned(blocks3, stage5, 0))
    other.append(swap(own[1], blocks3[:1]))
    other.append(swap(own[2], blocks3[:1]))
    other.append(swap(own[3][:2]) + swap(own[3][2:]))
    shared = (own, other, weights, factors, other_down, index)
    every = (0, 1, 2, 3)
    other.append(swap(own[3]))
    return project(every, every, *shared, None, (residual, gate, None))


def solution(mesh):
    shape = dict(mesh.shape)
    line = shape["seq"] == 4 and shape["img"] == 2 and shape["group"] == 2 and shape["tp"] == 2

    def shards(*arrays):
        image_count = arrays[0].shape[0]
        slots = arrays[9].shape[0]
        if line and image_count == 4 and slots == 4:
            return line_shards(*arrays)
        return general_shards(*arrays)

    return jax.shard_map(
        shards,
        mesh=mesh,
        in_specs=(
            P(("group", "img"), "seq", "tp"),
            P(("group", "img"), "seq", "tp"),
            P(("group", "img"), "seq", "tp"),
            P(("group", "img"), "seq", "tp"),
            P(("group", "img"), "tp"),
            P("tp", "seq"),
            P(("group", "seq", "img"), "tp", None),
            P(("group", "seq", "img"), None, "tp"),
            P("group"),
            P("group"),
            P("group"),
        ),
        out_specs=P(("group", "img"), "seq", "tp"),
        check_vma=False,
    )
```
